512 devices in a mesh: group: 8 (over y), dev: 64 (over x, z, core).
Axes of the slice: x: 4, y: 8, z: 8, core: 2. Of those that a mesh axis runs over, the one named last changes fastest.
Arguments:
- embeddings: float32 [524288, 256], P(('group', 'dev')), may hold values from -1.5 to 1.5
- adagrad_state: float32 [524288], P(('group', 'dev')), may hold values from 0.001 to 0.1
- relations: float32 [4, 256], replicated, may hold values from 0.1 to 1.9
- src_rows: int32 [2, 524288], P(None, ('group', 'dev')), may hold values from 0 to 1023
- rel_ids: int32 [2, 524288], P(None, ('group', 'dev')), may hold values from 0 to 3
- dst_slots: int32 [2, 524288], P(None, ('group', 'dev')), may hold values from 0 to 2047
- live_counts: int32 [2, 512], P(None, ('group', 'dev')), may hold values from 1 to 1024, 174592 in all within a row
- request_rows: int32 [2, 1048576], P(None, ('group', 'dev')), may hold values from 0 to 1023
Outputs:
- updated_embeddings: float32 [524288, 256], P(('group', 'dev'))
- updated_state: float32 [524288], P(('group', 'dev'))
The draws below stay inside these ranges and needn't reach their ends.
Inputs may be any that keep to these rules, and one draw needn't show every extreme that they name: `live_counts`: in every bucket one device has exactly 1024 live edges, and the live edges of all devices sum to the same total in every bucket.
All inputs are finite; a program needn't handle non-finite values.
Results may differ from the reference program's by a relative error of at most 0.0034.
Values may be sent and summed in bfloat16 or wider, within the bound.
A program may use at most 64 MiB of HBM per device.

```python
import math
import jax
import jax.numpy as jnp
import numpy as np
from jax import lax

D = 256
NREL = 4
BUCKETS = 2
RD = 1024
E_MAX = 1024
FETCH = 2048
CAP = 32
ENTITIES = 524288
N_GROUP = 8
N_DEV = 64
DEVICES = 512


def with_ends(entries, stream_key, low, largest):
    place = [jax.random.randint(jax.random.fold_in(stream_key, axis), (), 0, length) for axis, length in enumerate(entries.shape)]
    longest = entries.shape.index(max(entries.shape))
    neighbour = place[:longest] + [(place[longest] + 1) % entries.shape[longest]] + place[longest + 1:]
    return entries.at[tuple(place)].set(low).at[tuple(neighbour)].set(largest)


def block_scale(own_key, dims, cuts, smallest, largest):
    factor_of = 1.0
    for dim, shards_of in cuts:
        heights = jax.random.uniform(jax.random.fold_in(jax.random.fold_in(own_key, 6), dim), (shards_of,), jnp.float32, smallest / len(cuts), largest / len(cuts))
        factor_of = factor_of * jnp.repeat(jnp.exp(heights), dims[dim] // shards_of).reshape((-1,) + (1,) * (len(dims) - 1 - dim))
    return factor_of


def length_profile(amount, total, limit, lean):
    loads = [(1 << 20) // math.isqrt(standing ** lean) + 1 for standing in range(2, amount + 1)]
    rest, holding = total - limit - (amount - 1), [1] * (amount - 1)
    while rest > 0:
        movable = [i for i in range(amount - 1) if holding[i] < limit]
        whole, budget = sum([loads[i] for i in movable]), rest
        for i in movable:
            more = min(limit - holding[i], max(1, budget * loads[i] // whole), rest)
            holding[i] = holding[i] + more
            rest = rest - more
    return np.array([limit] + holding)


def ragged_sizes(stream_key, amount, total, reach, lean):
    if amount == 2:
        one = jax.random.randint(stream_key, (), max(1, total - reach), min(reach, total - 1) + 1)
        return jnp.stack([one, total - one])
    sizes = jnp.asarray(length_profile(amount, total, reach, lean), jnp.int32)
    couples = (amount - 1) // 2
    donor, receiver = sizes[1:1 + 2 * couples:2], sizes[2:2 + 2 * couples:2]
    slack = jnp.minimum(donor - 1, reach - receiver)
    passed = jax.random.randint(jax.random.fold_in(stream_key, 1), (couples,), 0, 1 << 20) % (slack + 1)
    sizes = sizes.at[1:1 + 2 * couples:2].set(donor - passed).at[2:2 + 2 * couples:2].set(receiver + passed)
    return sizes[jax.random.permutation(jax.random.fold_in(stream_key, 2), amount)]


def centred(rng, shape, spread, reach, split=(), kind=jnp.bfloat16):
    result = spread * jax.random.normal(rng, shape, jnp.float32)
    if split:
        result = result * block_scale(rng, shape, split, -0.22, 0.18)
    return jnp.clip(result, -reach, reach).astype(kind)


def setup_inputs(seed: int = 0) -> dict:
    seeds = jax.random.split(jax.random.key(seed), 9)
    embeddings = centred(seeds[0], (ENTITIES, D), 0.25, 1.5, ((0, 512),), jnp.float32)
    adagrad_state = jnp.clip(jnp.exp(math.log(0.1) - 4.6051702 * jax.random.uniform(seeds[1], (ENTITIES,), jnp.float32) ** block_scale(seeds[1], (ENTITIES,), ((0, 512),), -0.2, 0.2)), 0.001, 0.1)
    relations = jnp.clip(1.0 + 0.18 * jax.random.normal(seeds[2], (NREL, D), jnp.float32), 0.1, 1.9)
    src_rows = with_ends(jax.random.randint(seeds[3], (BUCKETS, DEVICES * E_MAX), 0, RD), jax.random.fold_in(seeds[3], 1), 0, RD - 1).astype(jnp.int32)
    rel_ids = with_ends(jax.random.randint(seeds[4], (BUCKETS, DEVICES * E_MAX), 0, NREL), jax.random.fold_in(seeds[4], 1), 0, NREL - 1).astype(jnp.int32)
    dst_slots = with_ends(jax.random.randint(seeds[5], (BUCKETS, DEVICES * E_MAX), 0, FETCH), jax.random.fold_in(seeds[5], 1), 0, FETCH - 1).astype(jnp.int32)
    live_counts = jax.vmap(lambda own: ragged_sizes(own, DEVICES, DEVICES * (E_MAX // 3), E_MAX, 2))(jax.random.split(seeds[6], BUCKETS)).reshape((BUCKETS, DEVICES)).astype(jnp.int32)
    request_rows = with_ends(jax.random.randint(seeds[7], (BUCKETS, DEVICES * FETCH), 0, RD), jax.random.fold_in(seeds[7], 1), 0, RD - 1).astype(jnp.int32)
    return {"embeddings": embeddings, "adagrad_state": adagrad_state, "relations": relations, "src_rows": src_rows, "rel_ids": rel_ids, "dst_slots": dst_slots, "live_counts": live_counts, "request_rows": request_rows}


learn_rate = 0.1
adagrad_eps = 1e-10

def edge_terms(current, fetched, relations, sources, relation_ids, targets, live_total):
    picks = (relation_ids[:, None] == jnp.arange(NREL)[None, :]).astype(jnp.float32)
    rel_rows = jnp.dot(picks, relations, precision=lax.Precision.HIGHEST)
    queries = (jnp.take(current, sources, axis=0) * rel_rows).astype(jnp.bfloat16)
    scores = jnp.dot(queries, fetched.T, preferred_element_type=jnp.float32)
    target_hit = targets[:, None] == jnp.arange(FETCH)[None, :]
    positive = lax.optimization_barrier(jnp.sum(jnp.where(target_hit, scores, 0.0), axis=1))
    live_mask = (jnp.arange(E_MAX) < live_total).astype(jnp.float32)
    coefficient = live_mask[:, None] * jax.nn.sigmoid(scores) / FETCH
    pulled = live_mask * jax.nn.sigmoid(-positive)
    coefficient = coefficient - jnp.where(target_hit, pulled[:, None], 0.0)
    coefficient = coefficient.astype(jnp.bfloat16)
    grad_query = jnp.dot(coefficient, fetched, preferred_element_type=jnp.float32)
    grad_fetched = jnp.dot(coefficient.T, queries, preferred_element_type=jnp.float32)
    source_grads = jax.ops.segment_sum(grad_query * rel_rows, sources, num_segments=RD)
    return (source_grads, grad_fetched)

def reference(embeddings, adagrad_state, relations, src_rows, rel_ids, dst_slots, live_counts, request_rows):
    devices = N_GROUP * N_DEV
    current = embeddings.reshape(devices, RD, D)
    row_state = adagrad_state.reshape(devices * RD)
    for bucket in range(BUCKETS):
        offset = 1 + bucket % (N_GROUP - 1)
        rounded = current.astype(jnp.bfloat16).reshape(N_GROUP, N_DEV, RD, D)
        sources = src_rows[bucket].reshape(devices, E_MAX)
        relation_ids = rel_ids[bucket].reshape(devices, E_MAX)
        targets = dst_slots[bucket].reshape(devices, E_MAX)
        requests = request_rows[bucket].reshape(devices, N_DEV, CAP)
        live_all = live_counts[bucket]

        def one_device(device_index):
            owner_group = (device_index // N_DEV - offset) % N_GROUP
            owner_rows = rounded[owner_group]
            fetched = owner_rows[jnp.arange(N_DEV)[:, None], requests[device_index]].reshape(FETCH, D)
            return edge_terms(current[device_index], fetched, relations, sources[device_index], relation_ids[device_index], targets[device_index], live_all[device_index])
        source_grads, fetched_grads = lax.map(one_device, jnp.arange(devices, dtype=jnp.int32))
        owner_base = (jnp.arange(devices, dtype=jnp.int32) // N_DEV - offset) % N_GROUP * N_DEV
        owner_device = owner_base[:, None] + jnp.arange(N_DEV, dtype=jnp.int32)[None, :]
        global_rows = (owner_device[:, :, None] * RD + requests).reshape(-1).astype(jnp.int32)
        dest_grads = jax.ops.segment_sum(fetched_grads.reshape(devices * FETCH, D), global_rows, num_segments=devices * RD)
        grads = source_grads.reshape(devices * RD, D) + dest_grads
        square = lax.optimization_barrier(jnp.mean(grads * grads, axis=1))
        row_state = row_state + square
        updated = current.reshape(devices * RD, D) - learn_rate * grads / (jnp.sqrt(row_state)[:, None] + adagrad_eps)
        current = updated.reshape(devices, RD, D)
    return (current.reshape(devices * RD, D), row_state)
```

```python
import functools

import jax
import jax.numpy as jnp
from jax import lax
from jax.experimental import pallas as pl
from jax.experimental.pallas import tpu as pltpu
from jax.sharding import PartitionSpec as P

MESH = pl.DeviceIdType.MESH
learn_rate = 0.1
adagrad_eps = 1e-10

NX, NZ, NC = 4, 8, 2
PEERS = NX * NZ * NC
ROWS, DIM = 1024, 256
EDGES, FETCH = 1024, 2048
CAP = FETCH // PEERS
STEP = 256
SLOTS = STEP // CAP
STEPS = FETCH // STEP
TILE = 256
BF16, F32 = jnp.bfloat16, jnp.float32


def disp(j):
    a, b = j // NZ, j % NZ
    u = (a + b) % (NX * NC)
    return u // NC, b, u % NC


def column(row):
    return jnp.broadcast_to(row, (128, 128)).T


def lanes(shape, start=0):
    return lax.broadcasted_iota(jnp.int32, shape, 1) + start


def subs(shape, start=0):
    return lax.broadcasted_iota(jnp.int32, shape, 0) + start


def one_hot_rows(rows):
    tiles = []
    for row in rows:
        col = column(row)
        tiles.append(
            jnp.concatenate(
                [(col == lanes((128, 128), 128 * t)).astype(F32).astype(BF16) for t in range(ROWS // 128)], axis=1
            )
        )
    return jnp.concatenate(tiles, axis=0)


def one_hot_columns(rows, start, count):
    place = subs((count, 128), start)
    return jnp.concatenate(
        [(place == jnp.broadcast_to(row, (count, 128))).astype(F32).astype(BF16) for row in rows], axis=1
    )


def dot(a, b, dims=((1,), (0,))):
    return lax.dot_general(a, b, (dims, ((), ())), preferred_element_type=F32)


def kernel(
    offsets,
    table_in, state_in, relations, src_ref, rel_ref, dst_ref, live_ref, request_ref,
    table, state_out,
    state, split, relrow, query, dstcol, gradq, total,
    ask, asked, packed,
    served, fetched, gradf, returned,
    ask_sent, ask_here, serve_sent, serve_here, return_sent, return_here,
):
    groups = lax.axis_size("group")
    g, d = lax.axis_index("group"), lax.axis_index("dev")
    mx, mz, mc = d // (NZ * NC), (d // NC) % NZ, d % NC

    def toward(j):
        x, z, c = disp(j)
        return ((mx + x) % NX) * (NZ * NC) + ((mz + z) % NZ) * NC + (mc + c) % NC

    def back(j):
        x, z, c = disp(j)
        return ((mx + NX - x) % NX) * (NZ * NC) + ((mz + NZ - z) % NZ) * NC + (mc + NC - c) % NC

    def rows_of(ref, j):
        return ref.at[pl.ds(pl.multiple_of(j * CAP, CAP), CAP)]

    def send(src, dst, sent, here, group, dev):
        pltpu.make_async_remote_copy(
            src_ref=src, dst_ref=dst, send_sem=sent, recv_sem=here, device_id=(group, dev), device_id_type=MESH
        ).start()

    def landed(ref, sem):
        pltpu.make_async_copy(ref, ref, sem).wait()

    barrier = pltpu.get_barrier_semaphore()

    def greet(j, carry):
        for s in offsets:
            for other in (s, groups - s):
                pl.semaphore_signal(barrier, 1, device_id=((g + other) % groups, j), device_id_type=MESH)
        return carry

    lax.fori_loop(0, PEERS, greet, 0)

    for b in range(len(offsets)):
        for r in range(FETCH // 128):
            row = request_ref[b : b + 1, 128 * r : 128 * (r + 1)]
            for u in range(4):
                turned = row if u == 0 else jnp.concatenate([row[:, 128 - CAP * u :], row[:, : 128 - CAP * u]], axis=1)
                ask[b, u, r] = turned

    pl.semaphore_wait(barrier, 2 * PEERS * len(offsets))

    for b, s in enumerate(offsets):

        def ask_owner(j, carry):
            owner = back(j)
            turn = (j % 4 + 4 - owner % 4) % 4
            send(
                ask.at[b, turn, owner // 4], asked.at[b, j], ask_sent.at[b], ask_here.at[b], (g + groups - s) % groups, owner
            )
            return carry

        lax.fori_loop(0, PEERS, ask_owner, 0)

    table[...] = table_in[...]
    for t in range(ROWS // 128):
        state[128 * t : 128 * (t + 1), :] = column(state_in[t : t + 1, :])

    for b, s in enumerate(offsets):
        ahead, behind = (g + s) % groups, (g + groups - s) % groups

        high = table[...].astype(BF16)
        split[:, :DIM] = high
        split[:, DIM:] = (table[...] - high.astype(F32)).astype(BF16)

        landed(asked.at[b], ask_here.at[b])
        lane = lanes((1, 128))
        for i in range(FETCH // 128):
            row = asked[b, 4 * i + 3]
            for m in (2, 1, 0):
                row = jnp.where(lane < CAP * (m + 1), asked[b, 4 * i + m], row)
            packed[b, i : i + 1, :] = row

        def serve(i, carry):
            ids = [packed[b, pl.ds(2 * i + h, 1), :] for h in range(2)]
            at = pl.ds(pl.multiple_of(i * STEP, STEP), STEP)
            served[b, at, :] = dot(one_hot_rows(ids), split[:, :DIM]).astype(BF16)

            def push(m, c):
                j = i * SLOTS + m
                send(
                    rows_of(served.at[b], j), rows_of(fetched.at[b], j), serve_sent.at[b], serve_here.at[b, i], ahead, toward(j)
                )
                return c

            lax.fori_loop(0, SLOTS, push, 0)
            return carry

        lax.fori_loop(0, STEPS, serve, 0)

        live = live_ref[b]
        edge = subs((EDGES // 128, 128)) * 128 + lanes((EDGES // 128, 128))
        source = jnp.where(edge < live, src_ref[b], -1)
        goal = dst_ref[b]
        owner = goal >> 5
        jz = (mz + NZ - ((owner >> 1) & (NZ - 1))) & (NZ - 1)
        ju = ((mx + NX - (owner >> 4)) & (NX - 1)) * NC + ((mc + NC - (owner & 1)) & 1)
        goal = ((((ju + NX * NC - jz) & (NX * NC - 1)) * NZ + jz) << 5) + (goal & (CAP - 1))
        kind = rel_ref[b]
        for t in range(EDGES // TILE):
            at = slice(t * TILE, (t + 1) * TILE)
            picks = [slice(2 * t + h, 2 * t + h + 1) for h in range(2)]
            rel = jnp.concatenate([column(kind[p, :]) for p in picks], axis=0)
            rel = jnp.concatenate([rel, rel], axis=1)
            wide = relations[0:1, :]
            for n in range(1, relations.shape[0]):
                wide = jnp.where(rel == n, relations[n : n + 1, :], wide)
            relrow[at, :] = wide
            both = dot(one_hot_rows([source[p, :] for p in picks]), split[...])
            query[at, :] = ((both[:, :DIM] + both[:, DIM:]) * wide).astype(BF16)
            dstcol[at, :] = jnp.concatenate([column(goal[p, :]) for p in picks], axis=0)
        gradq[...] = jnp.zeros_like(gradq)

        def score(i, carry):
            at = pl.ds(pl.multiple_of(i * STEP, STEP), STEP)
            landed(fetched.at[b, at], serve_here.at[b, i])
            rows = fetched[b, at, :]
            grads = jnp.zeros((STEP, DIM), F32)
            for t in range(EDGES // TILE):
                edges = slice(t * TILE, (t + 1) * TILE)
                q = query[edges, :]
                u = jnp.tanh(dot(q, rows, ((1,), (1,))) * 0.5)
                want = dstcol[edges, :] - i * STEP
                hit = jnp.concatenate([want == lanes((TILE, 128), 128 * h) for h in range(STEP // 128)], axis=1)
                a = 0.5 / FETCH
                coef = jnp.where(hit, u * (a + 0.5) + (a - 0.5), u * a + a).astype(BF16)
                gradq[edges, :] += dot(coef, rows)
                grads += dot(coef, q, ((0,), (0,)))
            gradf[b, at, :] = grads.astype(BF16)

            def push(m, c):
                j = i * SLOTS + m
                send(
                    rows_of(gradf.at[b], j), rows_of(returned.at[b], j), return_sent.at[b], return_here.at[b, i], behind, back(j)
                )
                return c

            lax.fori_loop(0, SLOTS, push, 0)
            return carry

        lax.fori_loop(0, STEPS, score, 0)

        whole = gradq[...] * relrow[...]
        top = whole.astype(BF16)
        parts = jnp.concatenate([top, (whole - top.astype(F32)).astype(BF16)], axis=1)
        for t in range(ROWS // TILE):
            at = slice(t * TILE, (t + 1) * TILE)
            spots = [source[r : r + 1, :] for r in range(EDGES // 128)]
            both = dot(one_hot_columns(spots, t * TILE, TILE), parts)
            total[at, :] = both[:, :DIM] + both[:, DIM:]

        def collect(i, carry):
            at = pl.ds(pl.multiple_of(i * STEP, STEP), STEP)
            landed(returned.at[b, at], return_here.at[b, i])
            ids = [packed[b, pl.ds(2 * i + h, 1), :] for h in range(2)]
            back_rows = returned[b, at, :]
            for t in range(ROWS // TILE):
                spot = slice(t * TILE, (t + 1) * TILE)
                total[spot, :] += dot(one_hot_columns(ids, t * TILE, TILE), back_rows)
            return carry

        lax.fori_loop(0, STEPS, collect, 0)

        for t in range(ROWS // TILE):
            at = slice(t * TILE, (t + 1) * TILE)
            grad = total[at, :]
            now = state[at, :] + jnp.mean(grad * grad, axis=1, keepdims=True)
            state[at, :] = now
            rate = learn_rate / (jnp.sqrt(now) + adagrad_eps)
            table[at, :] = table[at, :] - grad * jnp.concatenate([rate, rate], axis=1)

    for t in range(ROWS // 128):
        state_out[t : t + 1, :] = state[128 * t : 128 * (t + 1), :].T[0:1, :]

    for b in range(len(offsets)):
        landed(asked.at[b], ask_sent.at[b])
        landed(served.at[b], serve_sent.at[b])
        landed(gradf.at[b], return_sent.at[b])


def on_device(
    embeddings, adagrad_state, relations, src_rows, rel_ids, dst_slots, live_counts, request_rows
):
    groups = lax.axis_size("group")
    buckets = src_rows.shape[0]
    offsets = tuple(1 + b % (groups - 1) for b in range(buckets))
    blocks = (buckets, EDGES // 128, 128)
    vmem = pl.BlockSpec(memory_space=pltpu.VMEM)
    smem = pl.BlockSpec(memory_space=pltpu.SMEM)
    table, state = pl.pallas_call(
        functools.partial(kernel, offsets),
        out_shape=(
            jax.ShapeDtypeStruct((ROWS, DIM), F32),
            jax.ShapeDtypeStruct((ROWS // 128, 128), F32),
        ),
        in_specs=[vmem] * 6 + [smem, vmem],
        out_specs=(vmem, vmem),
        scratch_shapes=[
            pltpu.VMEM((ROWS, 128), F32),
            pltpu.VMEM((ROWS, 2 * DIM), BF16),
            pltpu.VMEM((EDGES, DIM), F32),
            pltpu.VMEM((EDGES, DIM), BF16),
            pltpu.VMEM((EDGES, 128), jnp.int32),
            pltpu.VMEM((EDGES, DIM), F32),
            pltpu.VMEM((ROWS, DIM), F32),
            pltpu.VMEM((buckets, 4, FETCH // 128, 1, 128), jnp.int32),
            pltpu.VMEM((buckets, PEERS, 1, 128), jnp.int32),
            pltpu.VMEM((buckets, FETCH // 128, 128), jnp.int32),
            pltpu.VMEM((buckets, FETCH, DIM), BF16),
            pltpu.VMEM((buckets, FETCH, DIM), BF16),
            pltpu.VMEM((buckets, FETCH, DIM), BF16),
            pltpu.VMEM((buckets, FETCH, DIM), BF16),
            pltpu.SemaphoreType.DMA((buckets,)),
            pltpu.SemaphoreType.DMA((buckets,)),
            pltpu.SemaphoreType.DMA((buckets,)),
            pltpu.SemaphoreType.DMA((buckets, STEPS)),
            pltpu.SemaphoreType.DMA((buckets,)),
            pltpu.SemaphoreType.DMA((buckets, STEPS)),
        ],
        compiler_params=pltpu.CompilerParams(
            collective_id=0, has_side_effects=True, vmem_limit_bytes=44 * 1024 * 1024
        ),
        name="bucket_pass",
    )(
        embeddings,
        adagrad_state.reshape(ROWS // 128, 128),
        relations,
        src_rows.reshape(blocks),
        rel_ids.reshape(blocks),
        dst_slots.reshape(blocks),
        live_counts.reshape(buckets),
        request_rows,
    )
    return table, state.reshape(ROWS)


def solution(mesh):
    return jax.shard_map(
        on_device,
        mesh=mesh,
        in_specs=(
            P(("group", "dev"), None),
            P(("group", "dev")),
            P(),
            P(None, ("group", "dev")),
            P(None, ("group", "dev")),
            P(None, ("group", "dev")),
            P(None, ("group", "dev")),
            P(None, ("group", "dev")),
        ),
        out_specs=(P(("group", "dev"), None), P(("group", "dev"))),
        check_vma=False,
    )
```

```python
import functools

import jax
import jax.numpy as jnp
from jax import lax
from jax.experimental import pallas as pl
from jax.experimental.pallas import tpu as pltpu
from jax.sharding import PartitionSpec as P

MESH = pl.DeviceIdType.MESH
learn_rate = 0.1
adagrad_eps = 1e-10

NX, NZ, NC = 4, 8, 2
PEERS = NX * NZ * NC
ROWS, DIM = 1024, 256
EDGES, FETCH = 1024, 2048
CAP = FETCH // PEERS
STEP = 256
SLOTS = STEP // CAP
STEPS = FETCH // STEP
TILE = 256
LEADS = (3, 3)
LAGS = (6, 0)
BF16, F32 = jnp.bfloat16, jnp.float32


def disp(a, b):
    u = (a + b) & (NX * NC - 1)
    return u // NC if isinstance(u, int) else u >> 1, b, u & (NC - 1)


def column(row):
    return jnp.broadcast_to(row, (128, 128)).T


def lanes(shape, start=0):
    return lax.broadcasted_iota(jnp.int32, shape, 1) + start


def subs(shape, start=0):
    return lax.broadcasted_iota(jnp.int32, shape, 0) + start


def one_hot_rows(rows):
    tiles = []
    for row in rows:
        col = column(row)
        tiles.append(
            jnp.concatenate(
                [(col == lanes((128, 128), 128 * t)).astype(F32).astype(BF16) for t in range(ROWS // 128)], axis=1
            )
        )
    return jnp.concatenate(tiles, axis=0)


def one_hot_columns(rows, start, count):
    place = subs((count, 128), start)
    return jnp.concatenate(
        [(place == jnp.broadcast_to(row, (count, 128))).astype(F32).astype(BF16) for row in rows], axis=1
    )


def dot(a, b, dims=((1,), (0,))):
    return lax.dot_general(a, b, (dims, ((), ())), preferred_element_type=F32)


def kernel(
    offsets,
    table_in, state_in, relations, src_ref, rel_ref, dst_ref, live_ref, request_ref,
    table, state_out,
    state, split, relrow, query, dstcol, gradq, total,
    ask, asked, packed,
    served, fetched, gradf, returned,
    ask_sent, ask_here, serve_sent, serve_here, return_sent, return_here,
):
    groups = lax.axis_size("group")
    g, d = lax.axis_index("group"), lax.axis_index("dev")
    mx, mz, mc = d // (NZ * NC), (d // NC) % NZ, d % NC

    def toward(a, b):
        x, z, c = disp(a, b)
        return ((mx + x) & (NX - 1)) * (NZ * NC) + ((mz + z) & (NZ - 1)) * NC + ((mc + c) & (NC - 1))

    def back(a, b):
        x, z, c = disp(a, b)
        return ((mx + NX - x) & (NX - 1)) * (NZ * NC) + ((mz + NZ - z) & (NZ - 1)) * NC + ((mc + NC - c) & (NC - 1))

    def rows_of(ref, j):
        return ref.at[pl.ds(pl.multiple_of(j * CAP, CAP), CAP)]

    def send(src, dst, sent, here, group, dev):
        pltpu.make_async_remote_copy(
            src_ref=src, dst_ref=dst, send_sem=sent, recv_sem=here, device_id=(group, dev), device_id_type=MESH
        ).start()

    def landed(ref, sem):
        pltpu.make_async_copy(ref, ref, sem).wait()

    barrier = pltpu.get_barrier_semaphore()

    def greet(j, carry):
        for s in offsets:
            for other in (s, groups - s):
                pl.semaphore_signal(barrier, 1, device_id=((g + other) % groups, j), device_id_type=MESH)
        return carry

    lax.fori_loop(0, PEERS, greet, 0)

    for b in range(len(offsets)):
        for r in range(FETCH // 128):
            row = request_ref[b : b + 1, 128 * r : 128 * (r + 1)]
            for u in range(4):
                turned = row if u == 0 else jnp.concatenate([row[:, 128 - CAP * u :], row[:, : 128 - CAP * u]], axis=1)
                ask[b, u, r] = turned

    pl.semaphore_wait(barrier, 2 * PEERS * len(offsets))

    def ask_owners(b):
        behind = (g + groups - offsets[b]) % groups

        def some(a, carry):
            for m in range(NZ):
                owner = back(a, m)
                turn = (m + 4 - (owner & 3)) & 3
                send(
                    ask.at[b, turn, owner >> 2], asked.at[b, a * NZ + m], ask_sent.at[b], ask_here.at[b], behind, owner
                )
            return carry

        lax.fori_loop(0, PEERS // NZ, some, 0)

    ask_owners(0)
    table[...] = table_in[...]
    for t in range(ROWS // 128):
        state[128 * t : 128 * (t + 1), :] = column(state_in[t : t + 1, :])

    for b, s in enumerate(offsets):
        lead, lag = LEADS[b], LAGS[b]
        ahead, behind = (g + s) % groups, (g + groups - s) % groups

        high = table[...].astype(BF16)
        split[:, :DIM] = high
        split[:, DIM:] = (table[...] - high.astype(F32)).astype(BF16)

        landed(asked.at[b], ask_here.at[b])
        lane = lanes((1, 128))
        for i in range(FETCH // 128):
            row = asked[b, 4 * i + 3]
            for m in (2, 1, 0):
                row = jnp.where(lane < CAP * (m + 1), asked[b, 4 * i + m], row)
            packed[b, i : i + 1, :] = row

        def push_served(i):
            for m in range(SLOTS):
                j = i * SLOTS + m
                send(
                    rows_of(served.at[b], j), rows_of(fetched.at[b], j), serve_sent.at[b], serve_here.at[b, i], ahead, toward(i, m)
                )

        def push_grads(i):
            for m in range(SLOTS):
                j = i * SLOTS + m
                send(
                    rows_of(gradf.at[b], j), rows_of(returned.at[b], j), return_sent.at[b], return_here.at[b, i], behind, back(i, m)
                )

        def serve(i, carry):
            ids = [packed[b, pl.ds(2 * i + h, 1), :] for h in range(2)]
            at = pl.ds(pl.multiple_of(i * STEP, STEP), STEP)
            served[b, at, :] = dot(one_hot_rows(ids), split[:, :DIM]).astype(BF16)


            @pl.when(i < lead)
            def _():
                push_served(i)

            return carry

        lax.fori_loop(0, STEPS, serve, 0)

        if b + 1 < len(offsets):
            ask_owners(b + 1)

        live = live_ref[b]
        edge = subs((EDGES // 128, 128)) * 128 + lanes((EDGES // 128, 128))
        source = jnp.where(edge < live, src_ref[b], -1)
        goal = dst_ref[b]
        owner = goal >> 5
        jz = (mz + NZ - ((owner >> 1) & (NZ - 1))) & (NZ - 1)
        ju = ((mx + NX - (owner >> 4)) & (NX - 1)) * NC + ((mc + NC - (owner & 1)) & 1)
        goal = ((((ju + NX * NC - jz) & (NX * NC - 1)) * NZ + jz) << 5) + (goal & (CAP - 1))
        kind = rel_ref[b]
        for t in range(EDGES // TILE):
            at = slice(t * TILE, (t + 1) * TILE)
            picks = [slice(2 * t + h, 2 * t + h + 1) for h in range(2)]
            rel = jnp.concatenate([column(kind[p, :]) for p in picks], axis=0)
            rel = jnp.concatenate([rel, rel], axis=1)
            wide = relations[0:1, :]
            for n in range(1, relations.shape[0]):
                wide = jnp.where(rel == n, relations[n : n + 1, :], wide)
            relrow[at, :] = wide
            both = dot(one_hot_rows([source[p, :] for p in picks]), split[...])
            query[at, :] = ((both[:, :DIM] + both[:, DIM:]) * wide).astype(BF16)
            dstcol[at, :] = jnp.concatenate([column(goal[p, :]) for p in picks], axis=0)
        gradq[...] = jnp.zeros_like(gradq)

        def score(i, carry):
            at = pl.ds(pl.multiple_of(i * STEP, STEP), STEP)
            landed(fetched.at[b, at], serve_here.at[b, i])

            @pl.when(i + lead < STEPS)
            def _():
                push_served(i + lead)

            rows = fetched[b, at, :]
            grads = jnp.zeros((STEP, DIM), F32)
            for t in range(EDGES // TILE):
                edges = slice(t * TILE, (t + 1) * TILE)
                q = query[edges, :]
                u = jnp.tanh(dot(q, rows, ((1,), (1,))) * 0.5)
                want = dstcol[edges, :] - i * STEP
                hit = jnp.concatenate([want == lanes((TILE, 128), 128 * h) for h in range(STEP // 128)], axis=1)
                a = 0.5 / FETCH
                coef = jnp.where(hit, u * (a + 0.5) + (a - 0.5), u * a + a).astype(BF16)
                gradq[edges, :] += dot(coef, rows)
                grads += dot(coef, q, ((0,), (0,)))
            gradf[b, at, :] = grads.astype(BF16)


            @pl.when(i >= lag)
            def _():
                push_grads(i - lag)

            return carry

        lax.fori_loop(0, STEPS, score, 0)
        for i in range(STEPS - lag, STEPS):
            push_grads(i)

        whole = gradq[...] * relrow[...]
        top = whole.astype(BF16)
        parts = jnp.concatenate([top, (whole - top.astype(F32)).astype(BF16)], axis=1)
        for t in range(ROWS // TILE):
            at = slice(t * TILE, (t + 1) * TILE)
            spots = [source[r : r + 1, :] for r in range(EDGES // 128)]
            both = dot(one_hot_columns(spots, t * TILE, TILE), parts)
            total[at, :] = both[:, :DIM] + both[:, DIM:]

        def collect(i, carry):
            at = pl.ds(pl.multiple_of(i * STEP, STEP), STEP)
            landed(returned.at[b, at], return_here.at[b, i])
            ids = [packed[b, pl.ds(2 * i + h, 1), :] for h in range(2)]
            back_rows = returned[b, at, :]
            for t in range(ROWS // TILE):
                spot = slice(t * TILE, (t + 1) * TILE)
                total[spot, :] += dot(one_hot_columns(ids, t * TILE, TILE), back_rows)
            return carry

        lax.fori_loop(0, STEPS, collect, 0)

        for t in range(ROWS // TILE):
            at = slice(t * TILE, (t + 1) * TILE)
            grad = total[at, :]
            now = state[at, :] + jnp.mean(grad * grad, axis=1, keepdims=True)
            state[at, :] = now
            rate = learn_rate / (jnp.sqrt(now) + adagrad_eps)
            table[at, :] = table[at, :] - grad * jnp.concatenate([rate, rate], axis=1)

    for t in range(ROWS // 128):
        state_out[t : t + 1, :] = state[128 * t : 128 * (t + 1), :].T[0:1, :]

    for b in range(len(offsets)):
        landed(asked.at[b], ask_sent.at[b])
        landed(served.at[b], serve_sent.at[b])
        landed(gradf.at[b], return_sent.at[b])


def on_device(
    embeddings, adagrad_state, relations, src_rows, rel_ids, dst_slots, live_counts, request_rows
):
    groups = lax.axis_size("group")
    buckets = src_rows.shape[0]
    offsets = tuple(1 + b % (groups - 1) for b in range(buckets))
    blocks = (buckets, EDGES // 128, 128)
    vmem = pl.BlockSpec(memory_space=pltpu.VMEM)
    smem = pl.BlockSpec(memory_space=pltpu.SMEM)
    table, state = pl.pallas_call(
        functools.partial(kernel, offsets),
        out_shape=(
            jax.ShapeDtypeStruct((ROWS, DIM), F32),
            jax.ShapeDtypeStruct((ROWS // 128, 128), F32),
        ),
        in_specs=[vmem] * 6 + [smem, vmem],
        out_specs=(vmem, vmem),
        scratch_shapes=[
            pltpu.VMEM((ROWS, 128), F32),
            pltpu.VMEM((ROWS, 2 * DIM), BF16),
            pltpu.VMEM((EDGES, DIM), F32),
            pltpu.VMEM((EDGES, DIM), BF16),
            pltpu.VMEM((EDGES, 128), jnp.int32),
            pltpu.VMEM((EDGES, DIM), F32),
            pltpu.VMEM((ROWS, DIM), F32),
            pltpu.VMEM((buckets, 4, FETCH // 128, 1, 128), jnp.int32),
            pltpu.VMEM((buckets, PEERS, 1, 128), jnp.int32),
            pltpu.VMEM((buckets, FETCH // 128, 128), jnp.int32),
            pltpu.VMEM((buckets, FETCH, DIM), BF16),
            pltpu.VMEM((buckets, FETCH, DIM), BF16),
            pltpu.VMEM((buckets, FETCH, DIM), BF16),
            pltpu.VMEM((buckets, FETCH, DIM), BF16),
            pltpu.SemaphoreType.DMA((buckets,)),
            pltpu.SemaphoreType.DMA((buckets,)),
            pltpu.SemaphoreType.DMA((buckets,)),
            pltpu.SemaphoreType.DMA((buckets, STEPS)),
            pltpu.SemaphoreType.DMA((buckets,)),
            pltpu.SemaphoreType.DMA((buckets, STEPS)),
        ],
        compiler_params=pltpu.CompilerParams(
            collective_id=0, has_side_effects=True, vmem_limit_bytes=44 * 1024 * 1024
        ),
        name="bucket_pass",
    )(
        embeddings,
        adagrad_state.reshape(ROWS // 128, 128),
        relations,
        src_rows.reshape(blocks),
        rel_ids.reshape(blocks),
        dst_slots.reshape(blocks),
        live_counts.reshape(buckets),
        request_rows,
    )
    return table, state.reshape(ROWS)


def solution(mesh):
    return jax.shard_map(
        on_device,
        mesh=mesh,
        in_specs=(
            P(("group", "dev"), None),
            P(("group", "dev")),
            P(),
            P(None, ("group", "dev")),
            P(None, ("group", "dev")),
            P(None, ("group", "dev")),
            P(None, ("group", "dev")),
            P(None, ("group", "dev")),
        ),
        out_specs=(P(("group", "dev"), None), P(("group", "dev"))),
        check_vma=False,
    )
```

```python
import functools

import jax
import jax.numpy as jnp
from jax import lax
from jax.experimental import pallas as pl
from jax.experimental.pallas import tpu as pltpu
from jax.sharding import PartitionSpec as P

MESH = pl.DeviceIdType.MESH
learn_rate = 0.1
adagrad_eps = 1e-10

NX, NZ, NC = 4, 8, 2
PEERS = NX * NZ * NC
ROWS, DIM = 1024, 256
EDGES, FETCH = 1024, 2048
CAP = FETCH // PEERS
STEP = 256
SLOTS = STEP // CAP
STEPS = FETCH // STEP
TILE = 256
LEADS = (3, 3)
LAGS = (5, 0)
BF16, F32 = jnp.bfloat16, jnp.float32


def disp(a, b):
    u = (a + b) & (NX * NC - 1)
    return u // NC if isinstance(u, int) else u >> 1, b, u & (NC - 1)


def column(row):
    return jnp.broadcast_to(row, (128, 128)).T


def lanes(shape, start=0):
    return lax.broadcasted_iota(jnp.int32, shape, 1) + start


def subs(shape, start=0):
    return lax.broadcasted_iota(jnp.int32, shape, 0) + start


def one_hot_rows(rows):
    tiles = []
    for row in rows:
        col = column(row)
        tiles.append(
            jnp.concatenate(
                [(col == lanes((128, 128), 128 * t)).astype(F32).astype(BF16) for t in range(ROWS // 128)], axis=1
            )
        )
    return jnp.concatenate(tiles, axis=0)


def one_hot_columns(rows, start, count):
    place = subs((count, 128), start)
    return jnp.concatenate(
        [(place == jnp.broadcast_to(row, (count, 128))).astype(F32).astype(BF16) for row in rows], axis=1
    )


def dot(a, b, dims=((1,), (0,))):
    return lax.dot_general(a, b, (dims, ((), ())), preferred_element_type=F32)


def kernel(
    offsets,
    table_in, state_in, relations_in, src_in, rel_in, dst_in, live_in, request_in,
    table, state_out,
    relations, state_rows, src_ref, rel_ref, dst_ref, live_ref, request_ref, load_sem,
    state, split, relrow, query, dstcol, gradq, total,
    ask, asked, packed,
    served, fetched, gradf, returned,
    ask_sent, ask_here, serve_sent, serve_here, return_sent, return_here,
):
    groups = lax.axis_size("group")
    g, d = lax.axis_index("group"), lax.axis_index("dev")
    mx, mz, mc = d // (NZ * NC), (d // NC) % NZ, d % NC

    def toward(a, b):
        x, z, c = disp(a, b)
        return ((mx + x) & (NX - 1)) * (NZ * NC) + ((mz + z) & (NZ - 1)) * NC + ((mc + c) & (NC - 1))

    def back(a, b):
        x, z, c = disp(a, b)
        return ((mx + NX - x) & (NX - 1)) * (NZ * NC) + ((mz + NZ - z) & (NZ - 1)) * NC + ((mc + NC - c) & (NC - 1))

    def rows_of(ref, j):
        return ref.at[pl.ds(pl.multiple_of(j * CAP, CAP), CAP)]

    def send(src, dst, sent, here, group, dev):
        pltpu.make_async_remote_copy(
            src_ref=src, dst_ref=dst, send_sem=sent, recv_sem=here, device_id=(group, dev), device_id_type=MESH
        ).start()

    def landed(ref, sem):
        pltpu.make_async_copy(ref, ref, sem).wait()

    barrier = pltpu.get_barrier_semaphore()

    def greet(j, carry):
        for s in offsets:
            for other in (s, groups - s):
                pl.semaphore_signal(barrier, 1, device_id=((g + other) % groups, j), device_id_type=MESH)
        return carry

    loads = [
        pltpu.make_async_copy(src, dst, load_sem.at[n])
        for n, (src, dst) in enumerate([
            (request_in, request_ref), (table_in, table), (state_in, state_rows), (relations_in, relations),
            (src_in, src_ref), (rel_in, rel_ref), (dst_in, dst_ref), (live_in, live_ref),
        ])
    ]
    for load in loads:
        load.start()
    lax.fori_loop(0, PEERS, greet, 0)
    loads[0].wait()

    for b in range(len(offsets)):
        for r in range(FETCH // 128):
            row = request_ref[b : b + 1, 128 * r : 128 * (r + 1)]
            for u in range(4):
                turned = row if u == 0 else jnp.concatenate([row[:, 128 - CAP * u :], row[:, : 128 - CAP * u]], axis=1)
                ask[b, u, r] = turned

    pl.semaphore_wait(barrier, 2 * PEERS * len(offsets))

    def ask_owners(b):
        behind = (g + groups - offsets[b]) % groups

        def some(a, carry):
            for m in range(NZ):
                owner = back(a, m)
                turn = (m + 4 - (owner & 3)) & 3
                send(
                    ask.at[b, turn, owner >> 2], asked.at[b, a * NZ + m], ask_sent.at[b], ask_here.at[b], behind, owner
                )
            return carry

        lax.fori_loop(0, PEERS // NZ, some, 0)

    ask_owners(0)
    for load in loads[1:]:
        load.wait()
    for t in range(ROWS // 128):
        state[128 * t : 128 * (t + 1), :] = column(state_rows[t : t + 1, :])

    for b, s in enumerate(offsets):
        lead, lag = LEADS[b], LAGS[b]
        ahead, behind = (g + s) % groups, (g + groups - s) % groups

        high = table[...].astype(BF16)
        split[:, :DIM] = high
        split[:, DIM:] = (table[...] - high.astype(F32)).astype(BF16)

        def queries():
            live = jnp.broadcast_to(live_ref[0:1, b : b + 1], (EDGES // 128, 128))

            def table_of(ref):
                return jnp.concatenate([ref[b : b + 1, 128 * r : 128 * (r + 1)] for r in range(EDGES // 128)], axis=0)

            edge = subs((EDGES // 128, 128)) * 128 + lanes((EDGES // 128, 128))
            source = jnp.where(edge < live, table_of(src_ref), -1)
            goal = table_of(dst_ref)
            owner = goal >> 5
            jz = (mz + NZ - ((owner >> 1) & (NZ - 1))) & (NZ - 1)
            ju = ((mx + NX - (owner >> 4)) & (NX - 1)) * NC + ((mc + NC - (owner & 1)) & 1)
            goal = ((((ju + NX * NC - jz) & (NX * NC - 1)) * NZ + jz) << 5) + (goal & (CAP - 1))
            kind = table_of(rel_ref)
            for t in range(EDGES // TILE):
                at = slice(t * TILE, (t + 1) * TILE)
                picks = [slice(2 * t + h, 2 * t + h + 1) for h in range(2)]
                rel = jnp.concatenate([column(kind[p, :]) for p in picks], axis=0)
                rel = jnp.concatenate([rel, rel], axis=1)
                wide = relations[0:1, :]
                for n in range(1, relations.shape[0]):
                    wide = jnp.where(rel == n, relations[n : n + 1, :], wide)
                relrow[at, :] = wide
                both = dot(one_hot_rows([source[p, :] for p in picks]), split[...])
                query[at, :] = ((both[:, :DIM] + both[:, DIM:]) * wide).astype(BF16)
                dstcol[at, :] = jnp.concatenate([column(goal[p, :]) for p in picks], axis=0)
            gradq[...] = jnp.zeros_like(gradq)
            return source

        if b == 0:
            source = queries()

        landed(asked.at[b], ask_here.at[b])
        lane = lanes((1, 128))
        for i in range(FETCH // 128):
            row = asked[b, 4 * i + 3]
            for m in (2, 1, 0):
                row = jnp.where(lane < CAP * (m + 1), asked[b, 4 * i + m], row)
            packed[b, i : i + 1, :] = row

        def push_served(i):
            for m in range(SLOTS):
                j = i * SLOTS + m
                send(
                    rows_of(served.at[b], j), rows_of(fetched.at[b], j), serve_sent.at[b], serve_here.at[b, i], ahead, toward(i, m)
                )

        def push_grads(i):
            for m in range(SLOTS):
                j = i * SLOTS + m
                send(
                    rows_of(gradf.at[b], j), rows_of(returned.at[b], j), return_sent.at[b], return_here.at[b, i], behind, back(i, m)
                )

        def serve(i, carry):
            ids = [packed[b, pl.ds(2 * i + h, 1), :] for h in range(2)]
            at = pl.ds(pl.multiple_of(i * STEP, STEP), STEP)
            served[b, at, :] = dot(one_hot_rows(ids), split[:, :DIM]).astype(BF16)


            @pl.when(i < lead)
            def _():
                push_served(i)

            return carry

        lax.fori_loop(0, STEPS, serve, 0)

        if b > 0:
            source = queries()

        def score(i, carry):
            at = pl.ds(pl.multiple_of(i * STEP, STEP), STEP)
            landed(fetched.at[b, at], serve_here.at[b, i])

            @pl.when(i + lead < STEPS)
            def _():
                push_served(i + lead)

            rows = fetched[b, at, :]
            grads = jnp.zeros((STEP, DIM), F32)
            for t in range(EDGES // TILE):
                edges = slice(t * TILE, (t + 1) * TILE)
                q = query[edges, :]
                u = jnp.tanh(dot(q, rows, ((1,), (1,))) * 0.5)
                want = dstcol[edges, :] - i * STEP
                hit = jnp.concatenate([want == lanes((TILE, 128), 128 * h) for h in range(STEP // 128)], axis=1)
                a = 0.5 / FETCH
                coef = jnp.where(hit, u * (a + 0.5) + (a - 0.5), u * a + a).astype(BF16)
                gradq[edges, :] += dot(coef, rows)
                grads += dot(coef, q, ((0,), (0,)))
            gradf[b, at, :] = grads.astype(BF16)


            @pl.when(i >= lag)
            def _():
                push_grads(i - lag)

            return carry

        lax.fori_loop(0, STEPS, score, 0)
        for i in range(STEPS - lag, STEPS):
            push_grads(i)

        if b + 1 < len(offsets):
            ask_owners(b + 1)

        whole = gradq[...] * relrow[...]
        top = whole.astype(BF16)
        parts = jnp.concatenate([top, (whole - top.astype(F32)).astype(BF16)], axis=1)
        for t in range(ROWS // TILE):
            at = slice(t * TILE, (t + 1) * TILE)
            spots = [source[r : r + 1, :] for r in range(EDGES // 128)]
            both = dot(one_hot_columns(spots, t * TILE, TILE), parts)
            total[at, :] = both[:, :DIM] + both[:, DIM:]

        def collect(i, carry):
            at = pl.ds(pl.multiple_of(i * STEP, STEP), STEP)
            landed(returned.at[b, at], return_here.at[b, i])
            ids = [packed[b, pl.ds(2 * i + h, 1), :] for h in range(2)]
            back_rows = returned[b, at, :]
            for t in range(ROWS // TILE):
                spot = slice(t * TILE, (t + 1) * TILE)
                total[spot, :] += dot(one_hot_columns(ids, t * TILE, TILE), back_rows)
            return carry

        lax.fori_loop(0, STEPS, collect, 0)

        for t in range(ROWS // TILE):
            at = slice(t * TILE, (t + 1) * TILE)
            grad = total[at, :]
            now = state[at, :] + jnp.mean(grad * grad, axis=1, keepdims=True)
            state[at, :] = now
            rate = learn_rate / (jnp.sqrt(now) + adagrad_eps)
            table[at, :] = table[at, :] - grad * jnp.concatenate([rate, rate], axis=1)

    for t in range(ROWS // 128):
        state_out[t : t + 1, :] = state[128 * t : 128 * (t + 1), :].T[0:1, :]

    for b in range(len(offsets)):
        landed(asked.at[b], ask_sent.at[b])
        landed(served.at[b], serve_sent.at[b])
        landed(gradf.at[b], return_sent.at[b])


def on_device(
    embeddings, adagrad_state, relations, src_rows, rel_ids, dst_slots, live_counts, request_rows
):
    groups = lax.axis_size("group")
    buckets = src_rows.shape[0]
    offsets = tuple(1 + b % (groups - 1) for b in range(buckets))
    vmem = pl.BlockSpec(memory_space=pltpu.VMEM)
    hbm = pl.BlockSpec(memory_space=pltpu.HBM)
    table, state = pl.pallas_call(
        functools.partial(kernel, offsets),
        out_shape=(
            jax.ShapeDtypeStruct((ROWS, DIM), F32),
            jax.ShapeDtypeStruct((ROWS // 128, 128), F32),
        ),
        in_specs=[hbm] * 8,
        out_specs=(vmem, vmem),
        scratch_shapes=[
            pltpu.VMEM(relations.shape, F32),
            pltpu.VMEM((ROWS // 128, 128), F32),
            pltpu.VMEM((buckets, EDGES), jnp.int32),
            pltpu.VMEM((buckets, EDGES), jnp.int32),
            pltpu.VMEM((buckets, EDGES), jnp.int32),
            pltpu.VMEM((1, buckets), jnp.int32),
            pltpu.VMEM((buckets, FETCH), jnp.int32),
            pltpu.SemaphoreType.DMA((8,)),
            pltpu.VMEM((ROWS, 128), F32),
            pltpu.VMEM((ROWS, 2 * DIM), BF16),
            pltpu.VMEM((EDGES, DIM), F32),
            pltpu.VMEM((EDGES, DIM), BF16),
            pltpu.VMEM((EDGES, 128), jnp.int32),
            pltpu.VMEM((EDGES, DIM), F32),
            pltpu.VMEM((ROWS, DIM), F32),
            pltpu.VMEM((buckets, 4, FETCH // 128, 1, 128), jnp.int32),
            pltpu.VMEM((buckets, PEERS, 1, 128), jnp.int32),
            pltpu.VMEM((buckets, FETCH // 128, 128), jnp.int32),
            pltpu.VMEM((buckets, FETCH, DIM), BF16),
            pltpu.VMEM((buckets, FETCH, DIM), BF16),
            pltpu.VMEM((buckets, FETCH, DIM), BF16),
            pltpu.VMEM((buckets, FETCH, DIM), BF16),
            pltpu.SemaphoreType.DMA((buckets,)),
            pltpu.SemaphoreType.DMA((buckets,)),
            pltpu.SemaphoreType.DMA((buckets,)),
            pltpu.SemaphoreType.DMA((buckets, STEPS)),
            pltpu.SemaphoreType.DMA((buckets,)),
            pltpu.SemaphoreType.DMA((buckets, STEPS)),
        ],
        compiler_params=pltpu.CompilerParams(
            collective_id=0, has_side_effects=True, vmem_limit_bytes=62 * 1024 * 1024
        ),
        name="bucket_pass",
    )(
        embeddings,
        adagrad_state.reshape(ROWS // 128, 128),
        relations,
        src_rows,
        rel_ids,
        dst_slots,
        live_counts.reshape(1, buckets),
        request_rows,
    )
    return table, state.reshape(ROWS)


def solution(mesh):
    return jax.shard_map(
        on_device,
        mesh=mesh,
        in_specs=(
            P(("group", "dev"), None),
            P(("group", "dev")),
            P(),
            P(None, ("group", "dev")),
            P(None, ("group", "dev")),
            P(None, ("group", "dev")),
            P(None, ("group", "dev")),
            P(None, ("group", "dev")),
        ),
        out_specs=(P(("group", "dev"), None), P(("group", "dev"))),
        check_vma=False,
    )
```

```python
import functools

import jax
import jax.numpy as jnp
from jax import lax
from jax.experimental import pallas as pl
from jax.experimental.pallas import tpu as pltpu
from jax.sharding import PartitionSpec as P

MESH = pl.DeviceIdType.MESH
learn_rate = 0.1
adagrad_eps = 1e-10

NX, NZ, NC = 4, 8, 2
PEERS = NX * NZ * NC
ROWS, DIM = 1024, 256
EDGES, FETCH = 1024, 2048
CAP = FETCH // PEERS
STEP = 128
SLOTS = STEP // CAP
STEPS = FETCH // STEP
PER = NZ // SLOTS
TILE = 256
LEADS = (6, 6)
LAGS = (11, 0)
BF16, F32 = jnp.bfloat16, jnp.float32


def disp(a, b):
    u = (a + b) & (NX * NC - 1)
    return u // NC if isinstance(u, int) else u >> 1, b, u & (NC - 1)


def column(row):
    return jnp.broadcast_to(row, (128, 128)).T


def lanes(shape, start=0):
    return lax.broadcasted_iota(jnp.int32, shape, 1) + start


def subs(shape, start=0):
    return lax.broadcasted_iota(jnp.int32, shape, 0) + start


def one_hot_rows(rows):
    tiles = []
    for row in rows:
        col = column(row)
        tiles.append(
            jnp.concatenate(
                [(col == lanes((128, 128), 128 * t)).astype(F32).astype(BF16) for t in range(ROWS // 128)], axis=1
            )
        )
    return jnp.concatenate(tiles, axis=0)


def one_hot_columns(rows, start, count):
    place = subs((count, 128), start)
    return jnp.concatenate(
        [(place == jnp.broadcast_to(row, (count, 128))).astype(F32).astype(BF16) for row in rows], axis=1
    )


def dot(a, b, dims=((1,), (0,))):
    return lax.dot_general(a, b, (dims, ((), ())), preferred_element_type=F32)


def kernel(
    offsets,
    table_in, state_in, relations_in, src_in, rel_in, dst_in, live_in, request_in,
    table, state_out,
    relations, state_rows, src_ref, rel_ref, dst_ref, live_ref, request_ref, load_sem,
    state, split, relrow, query, dstcol, gradq, total,
    ask, asked, packed,
    served, fetched, gradf, returned,
    ask_sent, ask_here, serve_sent, serve_here, return_sent, return_here,
):
    groups = lax.axis_size("group")
    g, d = lax.axis_index("group"), lax.axis_index("dev")
    mx, mz, mc = d // (NZ * NC), (d // NC) % NZ, d % NC

    def toward(a, b):
        x, z, c = disp(a, b)
        return ((mx + x) & (NX - 1)) * (NZ * NC) + ((mz + z) & (NZ - 1)) * NC + ((mc + c) & (NC - 1))

    def back(a, b):
        x, z, c = disp(a, b)
        return ((mx + NX - x) & (NX - 1)) * (NZ * NC) + ((mz + NZ - z) & (NZ - 1)) * NC + ((mc + NC - c) & (NC - 1))

    def rows_of(ref, j):
        return ref.at[pl.ds(pl.multiple_of(j * CAP, CAP), CAP)]

    def send(src, dst, sent, here, group, dev):
        pltpu.make_async_remote_copy(
            src_ref=src, dst_ref=dst, send_sem=sent, recv_sem=here, device_id=(group, dev), device_id_type=MESH
        ).start()

    def landed(ref, sem):
        pltpu.make_async_copy(ref, ref, sem).wait()

    barrier = pltpu.get_barrier_semaphore()

    def greet(j, carry):
        for s in offsets:
            for other in (s, groups - s):
                pl.semaphore_signal(barrier, 1, device_id=((g + other) % groups, j), device_id_type=MESH)
        return carry

    loads = [
        pltpu.make_async_copy(src, dst, load_sem.at[n])
        for n, (src, dst) in enumerate([
            (request_in, request_ref), (table_in, table), (state_in, state_rows), (relations_in, relations),
            (src_in, src_ref), (rel_in, rel_ref), (dst_in, dst_ref), (live_in, live_ref),
        ])
    ]
    for load in loads:
        load.start()
    lax.fori_loop(0, PEERS, greet, 0)
    loads[0].wait()

    for b in range(len(offsets)):
        for r in range(FETCH // 128):
            row = request_ref[b : b + 1, 128 * r : 128 * (r + 1)]
            for u in range(4):
                turned = row if u == 0 else jnp.concatenate([row[:, 128 - CAP * u :], row[:, : 128 - CAP * u]], axis=1)
                ask[b, u, r] = turned

    pl.semaphore_wait(barrier, 2 * PEERS * len(offsets))

    def ask_owners(b):
        behind = (g + groups - offsets[b]) % groups

        def some(a, carry):
            for m in range(NZ):
                owner = back(a, m)
                turn = (m + 4 - (owner & 3)) & 3
                send(
                    ask.at[b, turn, owner >> 2], asked.at[b, a * NZ + m], ask_sent.at[b], ask_here.at[b], behind, owner
                )
            return carry

        lax.fori_loop(0, PEERS // NZ, some, 0)

    ask_owners(0)
    for load in loads[1:]:
        load.wait()
    for t in range(ROWS // 128):
        state[128 * t : 128 * (t + 1), :] = column(state_rows[t : t + 1, :])

    for b, s in enumerate(offsets):
        lead, lag = LEADS[b], LAGS[b]
        ahead, behind = (g + s) % groups, (g + groups - s) % groups

        high = table[...].astype(BF16)
        split[:, :DIM] = high
        split[:, DIM:] = (table[...] - high.astype(F32)).astype(BF16)

        def queries():
            live = jnp.broadcast_to(live_ref[0:1, b : b + 1], (EDGES // 128, 128))

            def table_of(ref):
                return jnp.concatenate([ref[b : b + 1, 128 * r : 128 * (r + 1)] for r in range(EDGES // 128)], axis=0)

            edge = subs((EDGES // 128, 128)) * 128 + lanes((EDGES // 128, 128))
            source = jnp.where(edge < live, table_of(src_ref), -1)
            goal = table_of(dst_ref)
            owner = goal >> 5
            jz = (mz + NZ - ((owner >> 1) & (NZ - 1))) & (NZ - 1)
            ju = ((mx + NX - (owner >> 4)) & (NX - 1)) * NC + ((mc + NC - (owner & 1)) & 1)
            goal = ((((ju + NX * NC - jz) & (NX * NC - 1)) * NZ + jz) << 5) + (goal & (CAP - 1))
            kind = table_of(rel_ref)
            for t in range(EDGES // TILE):
                at = slice(t * TILE, (t + 1) * TILE)
                picks = [slice(2 * t + h, 2 * t + h + 1) for h in range(2)]
                rel = jnp.concatenate([column(kind[p, :]) for p in picks], axis=0)
                rel = jnp.concatenate([rel, rel], axis=1)
                wide = relations[0:1, :]
                for n in range(1, relations.shape[0]):
                    wide = jnp.where(rel == n, relations[n : n + 1, :], wide)
                relrow[at, :] = wide
                both = dot(one_hot_rows([source[p, :] for p in picks]), split[...])
                query[at, :] = ((both[:, :DIM] + both[:, DIM:]) * wide).astype(BF16)
                dstcol[at, :] = jnp.concatenate([column(goal[p, :]) for p in picks], axis=0)
            gradq[...] = jnp.zeros_like(gradq)
            return source

        if b == 0:
            source = queries()

        landed(asked.at[b], ask_here.at[b])
        lane = lanes((1, 128))
        for i in range(FETCH // 128):
            row = asked[b, 4 * i + 3]
            for m in (2, 1, 0):
                row = jnp.where(lane < CAP * (m + 1), asked[b, 4 * i + m], row)
            packed[b, i : i + 1, :] = row

        def push_served(i):
            a, half = i // PER, i % PER * SLOTS
            for m in range(SLOTS):
                j = i * SLOTS + m
                send(
                    rows_of(served.at[b], j), rows_of(fetched.at[b], j), serve_sent.at[b], serve_here.at[b, i], ahead, toward(a, half + m)
                )

        def push_grads(i):
            a, half = i // PER, i % PER * SLOTS
            for m in range(SLOTS):
                j = i * SLOTS + m
                send(
                    rows_of(gradf.at[b], j), rows_of(returned.at[b], j), return_sent.at[b], return_here.at[b, i], behind, back(a, half + m)
                )

        def serve(i, carry):
            ids = [packed[b, pl.ds(STEP // 128 * i + h, 1), :] for h in range(STEP // 128)]
            at = pl.ds(pl.multiple_of(i * STEP, STEP), STEP)
            served[b, at, :] = dot(one_hot_rows(ids), split[:, :DIM]).astype(BF16)


            @pl.when(i < lead)
            def _():
                push_served(i)

            return carry

        lax.fori_loop(0, STEPS, serve, 0)

        if b > 0:
            source = queries()

        def score(i, carry):
            at = pl.ds(pl.multiple_of(i * STEP, STEP), STEP)
            landed(fetched.at[b, at], serve_here.at[b, i])

            @pl.when(i + lead < STEPS)
            def _():
                push_served(i + lead)

            rows = fetched[b, at, :]
            grads = jnp.zeros((STEP, DIM), F32)
            for t in range(EDGES // TILE):
                edges = slice(t * TILE, (t + 1) * TILE)
                q = query[edges, :]
                u = jnp.tanh(dot(q, rows, ((1,), (1,))) * 0.5)
                want = dstcol[edges, :] - i * STEP
                hit = jnp.concatenate([want == lanes((TILE, 128), 128 * h) for h in range(STEP // 128)], axis=1)
                a = 0.5 / FETCH
                coef = jnp.where(hit, u * (a + 0.5) + (a - 0.5), u * a + a).astype(BF16)
                gradq[edges, :] += dot(coef, rows)
                grads += dot(coef, q, ((0,), (0,)))
            gradf[b, at, :] = grads.astype(BF16)


            @pl.when(i >= lag)
            def _():
                push_grads(i - lag)

            return carry

        lax.fori_loop(0, STEPS, score, 0)
        for i in range(STEPS - lag, STEPS):
            push_grads(i)

        if b + 1 < len(offsets):
            ask_owners(b + 1)

        whole = gradq[...] * relrow[...]
        top = whole.astype(BF16)
        parts = jnp.concatenate([top, (whole - top.astype(F32)).astype(BF16)], axis=1)
        for t in range(ROWS // TILE):
            at = slice(t * TILE, (t + 1) * TILE)
            spots = [source[r : r + 1, :] for r in range(EDGES // 128)]
            both = dot(one_hot_columns(spots, t * TILE, TILE), parts)
            total[at, :] = both[:, :DIM] + both[:, DIM:]

        def collect(i, carry):
            at = pl.ds(pl.multiple_of(i * STEP, STEP), STEP)
            landed(returned.at[b, at], return_here.at[b, i])
            ids = [packed[b, pl.ds(STEP // 128 * i + h, 1), :] for h in range(STEP // 128)]
            back_rows = returned[b, at, :]
            for t in range(ROWS // TILE):
                spot = slice(t * TILE, (t + 1) * TILE)
                total[spot, :] += dot(one_hot_columns(ids, t * TILE, TILE), back_rows)
            return carry

        lax.fori_loop(0, STEPS, collect, 0)

        for t in range(ROWS // TILE):
            at = slice(t * TILE, (t + 1) * TILE)
            grad = total[at, :]
            now = state[at, :] + jnp.mean(grad * grad, axis=1, keepdims=True)
            state[at, :] = now
            rate = learn_rate / (jnp.sqrt(now) + adagrad_eps)
            table[at, :] = table[at, :] - grad * jnp.concatenate([rate, rate], axis=1)

    for t in range(ROWS // 128):
        state_out[t : t + 1, :] = state[128 * t : 128 * (t + 1), :].T[0:1, :]

    for b in range(len(offsets)):
        landed(asked.at[b], ask_sent.at[b])
        landed(served.at[b], serve_sent.at[b])
        landed(gradf.at[b], return_sent.at[b])


def on_device(
    embeddings, adagrad_state, relations, src_rows, rel_ids, dst_slots, live_counts, request_rows
):
    groups = lax.axis_size("group")
    buckets = src_rows.shape[0]
    offsets = tuple(1 + b % (groups - 1) for b in range(buckets))
    vmem = pl.BlockSpec(memory_space=pltpu.VMEM)
    hbm = pl.BlockSpec(memory_space=pltpu.HBM)
    table, state = pl.pallas_call(
        functools.partial(kernel, offsets),
        out_shape=(
            jax.ShapeDtypeStruct((ROWS, DIM), F32),
            jax.ShapeDtypeStruct((ROWS // 128, 128), F32),
        ),
        in_specs=[hbm] * 8,
        out_specs=(vmem, vmem),
        scratch_shapes=[
            pltpu.VMEM(relations.shape, F32),
            pltpu.VMEM((ROWS // 128, 128), F32),
            pltpu.VMEM((buckets, EDGES), jnp.int32),
            pltpu.VMEM((buckets, EDGES), jnp.int32),
            pltpu.VMEM((buckets, EDGES), jnp.int32),
            pltpu.VMEM((1, buckets), jnp.int32),
            pltpu.VMEM((buckets, FETCH), jnp.int32),
            pltpu.SemaphoreType.DMA((8,)),
            pltpu.VMEM((ROWS, 128), F32),
            pltpu.VMEM((ROWS, 2 * DIM), BF16),
            pltpu.VMEM((EDGES, DIM), F32),
            pltpu.VMEM((EDGES, DIM), BF16),
            pltpu.VMEM((EDGES, 128), jnp.int32),
            pltpu.VMEM((EDGES, DIM), F32),
            pltpu.VMEM((ROWS, DIM), F32),
            pltpu.VMEM((buckets, 4, FETCH // 128, 1, 128), jnp.int32),
            pltpu.VMEM((buckets, PEERS, 1, 128), jnp.int32),
            pltpu.VMEM((buckets, FETCH // 128, 128), jnp.int32),
            pltpu.VMEM((buckets, FETCH, DIM), BF16),
            pltpu.VMEM((buckets, FETCH, DIM), BF16),
            pltpu.VMEM((buckets, FETCH, DIM), BF16),
            pltpu.VMEM((buckets, FETCH, DIM), BF16),
            pltpu.SemaphoreType.DMA((buckets,)),
            pltpu.SemaphoreType.DMA((buckets,)),
            pltpu.SemaphoreType.DMA((buckets,)),
            pltpu.SemaphoreType.DMA((buckets, STEPS)),
            pltpu.SemaphoreType.DMA((buckets,)),
            pltpu.SemaphoreType.DMA((buckets, STEPS)),
        ],
        compiler_params=pltpu.CompilerParams(
            collective_id=0, has_side_effects=True, vmem_limit_bytes=62 * 1024 * 1024
        ),
        name="bucket_pass",
    )(
        embeddings,
        adagrad_state.reshape(ROWS // 128, 128),
        relations,
        src_rows,
        rel_ids,
        dst_slots,
        live_counts.reshape(1, buckets),
        request_rows,
    )
    return table, state.reshape(ROWS)


def solution(mesh):
    return jax.shard_map(
        on_device,
        mesh=mesh,
        in_specs=(
            P(("group", "dev"), None),
            P(("group", "dev")),
            P(),
            P(None, ("group", "dev")),
            P(None, ("group", "dev")),
            P(None, ("group", "dev")),
            P(None, ("group", "dev")),
            P(None, ("group", "dev")),
        ),
        out_specs=(P(("group", "dev"), None), P(("group", "dev"))),
        check_vma=False,
    )
```
